32 devices in a mesh: seq: 4 (over z), exp: 8 (over y, x, core).
Axes of the slice: x: 2, y: 2, z: 4, core: 2. Of those that a mesh axis runs over, the one named last changes fastest.
Arguments:
- queries: bfloat16 [512, 2048], P('seq', 'exp'), may hold values from -6 to 6
- key_matrix: bfloat16 [512, 2048], P('seq', 'exp'), may hold values from -6 to 6
- values: bfloat16 [512, 2048], P('seq', 'exp'), may hold values from -6 to 6
- log_decay: float32 [16, 512], P('exp', 'seq'), may hold values from -3 to 0
- residual: bfloat16 [512, 3072], P('seq'), may hold values from -6 to 6
- out_weight: bfloat16 [3072, 2048], P('seq', 'exp'), may hold values from -0.125 to 0.125
- router: bfloat16 [3072, 8], replicated, may hold values from -0.109375 to 0.109375
- expert_ids: int32 [512, 2], P('seq'), may hold values from 0 to 7, all different within a row; in each aligned block of 128 rows (0 to 127, 128 to 255, ...) at most 48 rows name the same one
- up_weight: bfloat16 [8, 3072, 4608], P('exp', None, 'seq'), may hold values from -0.109375 to 0.109375
- down_weight: bfloat16 [8, 4608, 3072], P('exp', 'seq'), may hold values from -0.09375 to 0.09375
Outputs:
- layer_out: bfloat16 [512, 3072], P(('seq', 'exp'))
The draws below stay inside these ranges and needn't reach their ends.
Inputs may be any that keep to these rules, and one draw needn't show every extreme that they name: `expert_ids`: in each aligned block of 128 rows (one sequence block) no expert is named by more than 48 rows, a bound that some block reaches; a row names 2 different experts.
All inputs are finite; a program needn't handle non-finite values.
Results may differ from the reference program's by a relative error of at most 0.015.
Values may be sent and summed in bfloat16 or wider, within the bound.
A program may use at most 64 MiB of HBM per device.

```python
import math
import jax
import jax.numpy as jnp
import numpy as np
from jax import lax

D = 3072
DH = 128
FFW = 4608
TOP = 2
BLK = 128
HEADS = 16
EXPERTS = 8
TOKENS = 512
CAP = 48
N_SEQ = 4


def draw_log_decay(key, part):
    keys = jax.random.split(key, 6)
    slow_share = 0.5
    slow = jax.random.bernoulli(keys[0], slow_share, (HEADS, 1))
    fast_rate = jnp.exp(jax.random.uniform(keys[1], (HEADS, 1), jnp.float32, math.log(1.0 / 50.0), math.log(1.0 / 30.0)))
    slow_rate = math.log(2.5) / TOKENS * jax.random.uniform(keys[2], (HEADS, 1), jnp.float32, 0.3, 1.0)
    decay_rate = jnp.where(slow, slow_rate, fast_rate)
    coarse_estimate = jax.random.uniform(keys[3], (HEADS, TOKENS), jnp.float32, 0.5, 1.5)
    slot_locations = jax.random.randint(keys[4], (HEADS, 3), 0, TOKENS)
    layer_depth = jax.random.uniform(keys[5], (HEADS, 3), jnp.float32, math.log(0.5), math.log(0.8))
    target_locations = jnp.arange(TOKENS, dtype=jnp.int32)[None, None, :]
    sudden_spike = jnp.sum(jnp.where(target_locations == slot_locations[:, :, None], layer_depth[:, :, None], 0.0), axis=1)
    return (-decay_rate * coarse_estimate + sudden_spike).astype(jnp.float32)


def levels(rng, dims, cuts, least, largest):
    gain, own = 1.0, jax.random.fold_in(rng, 6)
    for position, shards_of in cuts:
        draws = jnp.exp(jax.random.uniform(jax.random.fold_in(own, position), (shards_of,), jnp.float32, least / len(cuts), largest / len(cuts)))
        gain = gain * jnp.repeat(draws, dims[position] // shards_of).reshape([-1 if axis == position else 1 for axis in range(len(dims))])
    return gain


def routed_block(rng, own, number, rows, count, top, reach, lean):
    sequence = jax.random.permutation(rng, count)
    crowded, ordinary = load_shares(count, rows * top, reach, lean, True), load_shares(count, rows * top, reach, lean, False)
    places = jnp.arange(count)

    def named(tallies, turn):
        used = int((tallies > 0).sum())
        fixed = max(1, used // 4)
        moved = fixed + (places - fixed + turn * (used - fixed)) % max(1, count - fixed)
        return jnp.zeros((count,), jnp.int32).at[sequence[jnp.where(places < fixed, places, moved)]].set(jnp.asarray(tallies, jnp.int32))

    tallies = jnp.where(number % 4 == 0, named(crowded, number // 4), named(ordinary, number - number // 4 - 1))
    mixed = jax.random.permutation(jax.random.fold_in(own, 3), count)
    source_of, taker = mixed[0:count // 2 * 2:2], mixed[1:count // 2 * 2:2]
    slack = jnp.minimum(tallies[source_of] - 1, reach - tallies[taker]) // 2
    slack = jnp.where((source_of == sequence[0]) | (taker == sequence[0]) | (tallies[taker] == 0), 0, jnp.maximum(slack, 0))
    moved = jax.random.randint(jax.random.fold_in(own, 4), (count // 2,), 0, 1 << 20) % (slack + 1)
    tallies = tallies.at[source_of].add(-moved).at[taker].add(moved)
    labels = jnp.searchsorted(jnp.cumsum(tallies), jnp.arange(rows * top), side="right").astype(jnp.int32)
    grid = labels.reshape(top, rows).T
    grid = grid[jax.random.permutation(jax.random.fold_in(own, 1), rows)]
    turn = jax.random.randint(jax.random.fold_in(own, 2), (rows, 1), 0, top)
    return jnp.take_along_axis(grid, (jnp.arange(top)[None, :] + turn) % top, axis=1)


def load_shares(number_of, total, most, slope, full):
    weights = [(1 << 20) // math.isqrt(grade ** slope) + 1 for grade in range(1, number_of + 1)]
    largest = most if full else min(most, max(-(-total // number_of), total * weights[0] // sum(weights)))
    least = 1 if total - largest >= number_of - 1 else 0
    holding, spare = [largest] + [least] * (number_of - 1), total - largest - least * (number_of - 1)
    while spare > 0:
        free = [i for i in range(1, number_of) if holding[i] < largest] or [i for i in range(1, number_of) if holding[i] < most]
        mass, budget = sum([weights[i] for i in free]), spare
        for i in free:
            more = min(most - holding[i], max(1, budget * weights[i] // mass), spare)
            holding[i] = holding[i] + more
            spare = spare - more
    return np.array(holding)


def centred(rng, dims, spread, bound, cuts=(), kind=jnp.bfloat16):
    values = spread * jax.random.normal(rng, dims, jnp.float32)
    if cuts:
        values = values * levels(rng, dims, cuts, -0.22, 0.18)
    return jnp.clip(values, -bound, bound).astype(kind)


def setup_inputs(seed: int = 0) -> dict:
    splits = jax.random.split(jax.random.key(seed), 11)
    queries = centred(splits[0], (TOKENS, HEADS * DH), 1.0, 6.0, ((0, 4), (1, 8)))
    key_matrix = centred(splits[1], (TOKENS, HEADS * DH), 1.0, 6.0, ((0, 4), (1, 8)))
    values = centred(splits[2], (TOKENS, HEADS * DH), 1.0, 6.0, ((0, 4), (1, 8)))
    log_decay = draw_log_decay(jax.random.fold_in(splits[10], 71), 0)
    residual = centred(splits[4], (TOKENS, D), 1.0, 6.0, ((0, 4),))
    out_weight = centred(splits[5], (D, HEADS * DH), (HEADS * DH) ** -0.5, 0.125, ((0, 4), (1, 8)))
    router = centred(splits[6], (D, EXPERTS), D ** -0.5, 0.109375)
    expert_ids_keys = jax.random.split(jax.random.fold_in(splits[7], 1), TOKENS // BLK)
    expert_ids_turns = jax.random.permutation(jax.random.fold_in(splits[7], 3), TOKENS // BLK)
    expert_ids = jax.vmap(lambda own, number: routed_block(jax.random.fold_in(splits[7], 2), own, number, BLK, EXPERTS, TOP, CAP, 2))(expert_ids_keys, expert_ids_turns).reshape((TOKENS, TOP))
    up_weight = centred(splits[8], (EXPERTS, D, FFW), D ** -0.5, 0.109375, ((0, 8), (2, 4)))
    down_weight = centred(splits[9], (EXPERTS, FFW, D), FFW ** -0.5, 0.09375, ((0, 8), (1, 4)))
    return {"queries": queries, "key_matrix": key_matrix, "values": values, "log_decay": log_decay, "residual": residual, "out_weight": out_weight, "router": router, "expert_ids": expert_ids, "up_weight": up_weight, "down_weight": down_weight}


def block_step(state, inputs):
    qb, kb, vb, gb = inputs
    cum = jnp.cumsum(gb, axis=1)
    last = cum[:, -1:]
    size = gb.shape[1]
    lower = jnp.arange(size)[:, None] >= jnp.arange(size)[None, :]
    diff = cum[:, :, None] - cum[:, None, :]
    weight = jnp.where(lower[None], jnp.exp(jnp.where(lower[None], diff, 0.0)), 0.0)
    scores = jnp.einsum('hid,hjd->hij', qb, kb, precision=lax.Precision.HIGHEST) * weight
    inner = jnp.einsum('hij,hjd->hid', scores, vb, precision=lax.Precision.HIGHEST)
    outer = jnp.exp(cum)[:, :, None] * jnp.einsum('hid,hde->hie', qb, state, precision=lax.Precision.HIGHEST)
    kscaled = kb * jnp.exp(last - cum)[:, :, None]
    fresh = jnp.exp(last)[:, :, None] * state + jnp.einsum('hjd,hje->hde', kscaled, vb, precision=lax.Precision.HIGHEST)
    return (fresh, inner + outer)

def run_expert(operands):
    rows_e, up_e, down_e = operands
    hidden = jax.nn.silu(jnp.dot(rows_e, up_e, preferred_element_type=jnp.float32)).astype(jnp.bfloat16)
    return jnp.dot(hidden, down_e, preferred_element_type=jnp.float32)

def reference(queries, key_matrix, values, log_decay, residual, out_weight, router, expert_ids, up_weight, down_weight):

    def split_heads(array):
        return array.astype(jnp.float32).reshape(N_SEQ, BLK, HEADS, DH).transpose(0, 2, 1, 3)
    qall = split_heads(queries)
    kall = split_heads(key_matrix)
    vall = split_heads(values)
    decay = log_decay.reshape(HEADS, N_SEQ, BLK).transpose(1, 0, 2)
    start = jnp.zeros((HEADS, DH, DH), jnp.float32)
    _, mixed = lax.scan(block_step, start, (qall, kall, vall, decay))
    mixed = mixed * lax.rsqrt(lax.optimization_barrier(jnp.mean(mixed * mixed, axis=-1, keepdims=True)) + 1e-06)
    attn = mixed.transpose(0, 2, 1, 3).reshape(TOKENS, HEADS * DH).astype(jnp.bfloat16)
    projected = lax.dot_general(attn, out_weight, (((1,), (1,)), ((), ())), preferred_element_type=jnp.float32)
    stream = residual.astype(jnp.float32)
    normed = (stream * lax.rsqrt(lax.optimization_barrier(jnp.mean(stream * stream, axis=-1, keepdims=True)) + 1e-05)).astype(jnp.bfloat16)
    logits = jnp.dot(normed, router, preferred_element_type=jnp.float32)
    chosen = jnp.take_along_axis(logits, expert_ids, axis=1)
    score = jax.nn.sigmoid(chosen)
    gates = score / lax.optimization_barrier(jnp.sum(score, axis=1, keepdims=True))
    grouped = expert_ids.reshape(N_SEQ, BLK * TOP)
    onehot = (grouped[:, :, None] == jnp.arange(EXPERTS, dtype=jnp.int32)[None, None, :]).astype(jnp.int32)
    ranks = jnp.cumsum(onehot, axis=1) - onehot
    slot = lax.optimization_barrier(jnp.sum(ranks * onehot, axis=-1)).reshape(-1).astype(jnp.int32)
    flat_ids = expert_ids.reshape(-1).astype(jnp.int32)
    route = jnp.arange(TOKENS * TOP, dtype=jnp.int32)
    token_index = route // TOP
    row_index = token_index // BLK * CAP + slot
    buffer = jnp.zeros((EXPERTS, N_SEQ * CAP, D), jnp.bfloat16)
    buffer = buffer.at[flat_ids, row_index].set(normed[token_index])
    outputs = lax.map(run_expert, (buffer, up_weight, down_weight))
    picked = outputs[flat_ids, row_index].reshape(TOKENS, TOP, D)
    combined = lax.optimization_barrier(jnp.sum(gates[:, :, None] * picked, axis=1))
    return (stream + projected + combined).astype(jnp.bfloat16)
```

```python
import functools

import jax
import jax.numpy as jnp
from jax import lax
from jax.experimental import pallas as pl
from jax.experimental.pallas import tpu as pltpu
from jax.sharding import PartitionSpec as P

MESH = pl.DeviceIdType.MESH
F32 = jnp.float32
BF16 = jnp.bfloat16
EXACT = lax.Precision.HIGHEST


def tile_of(size, most):
    for width in range(most, 127, -128):
        if size % width == 0:
            return width
    return size


def layer(
    n,
    n_exp,
    cap,
    q_ref,
    k_ref,
    v_ref,
    decay_ref,
    res_ref,
    ow_ref,
    router_ref,
    ids_ref,
    up_hbm,
    down_hbm,
    out_ref,
    up,
    down,
    rows_buf,
    hidden,
    states,
    carried,
    attn_buf,
    stage,
    core_buf,
    half_buf,
    chip_buf,
    fin_send,
    fin_buf,
    load_sem,
    rows_s,
    rows_r,
    st_s,
    st_r,
    at_s,
    at_r,
    core_s,
    core_r,
    chip_s,
    chip_r,
    fin_s,
    fin_r,
):
    s = lax.axis_index("seq")
    e = lax.axis_index("exp")
    core = e % 2
    chip = e // 2
    chips = n_exp // 2
    partner = chip * 2 + 1 - core
    blk, width_d = res_ref.shape
    own = blk // n_exp
    heads = decay_ref.shape[0]
    dh = q_ref.shape[1] // heads
    cols = ow_ref.shape[0]

    load_up = pltpu.make_async_copy(up_hbm.at[0], up, load_sem.at[0])
    load_down = pltpu.make_async_copy(down_hbm.at[0], down, load_sem.at[1])
    load_up.start()
    load_down.start()

    barrier = pltpu.get_barrier_semaphore()

    @pl.loop(0, n)
    def _(j):
        @pl.when(j != s)
        def _():
            pl.semaphore_signal(barrier, inc=1, device_id=(j, e), device_id_type=MESH)

    @pl.loop(0, chips)
    def _(g):
        @pl.when(g != chip)
        def _():
            pl.semaphore_signal(
                barrier, inc=1, device_id=(s, g * 2 + core), device_id_type=MESH
            )

    pl.semaphore_signal(barrier, inc=1, device_id=(s, partner), device_id_type=MESH)

    def send_rows(b, way):
        return pltpu.make_async_remote_copy(
            src_ref=rows_buf.at[b],
            dst_ref=rows_buf.at[b],
            send_sem=rows_s.at[way, b],
            recv_sem=rows_r.at[b],
            device_id=((s + 1) % n if way == 0 else (s + n - 1) % n, e),
            device_id_type=MESH,
        )

    def send_state(to, slot):
        return pltpu.make_async_remote_copy(
            src_ref=states.at[slot],
            dst_ref=states.at[slot],
            send_sem=st_s.at[to],
            recv_sem=st_r.at[slot],
            device_id=(to, e),
            device_id_type=MESH,
        )

    def send_attn(to, slot):
        return pltpu.make_async_remote_copy(
            src_ref=attn_buf.at[slot],
            dst_ref=attn_buf.at[slot],
            send_sem=at_s.at[to],
            recv_sem=at_r.at[slot],
            device_id=(to, e),
            device_id_type=MESH,
        )

    def send_core(t):
        return pltpu.make_async_remote_copy(
            src_ref=stage.at[t, 1 - core],
            dst_ref=core_buf.at[t],
            send_sem=core_s.at[t],
            recv_sem=core_r.at[t],
            device_id=(s, partner),
            device_id_type=MESH,
        )

    def send_chip(t, to, slot):
        return pltpu.make_async_remote_copy(
            src_ref=half_buf.at[t, to],
            dst_ref=chip_buf.at[t, slot],
            send_sem=chip_s.at[t, to],
            recv_sem=chip_r.at[t, slot],
            device_id=(s, to * 2 + core),
            device_id_type=MESH,
        )

    def send_fin(t, to, slot):
        return pltpu.make_async_remote_copy(
            src_ref=fin_send.at[t],
            dst_ref=fin_buf.at[slot],
            send_sem=fin_s.at[t],
            recv_sem=fin_r.at[slot],
            device_id=(to, e),
            device_id_type=MESH,
        )

    stream = res_ref[...].astype(F32)
    normed = (
        stream * lax.rsqrt(jnp.mean(stream * stream, axis=-1, keepdims=True) + 1e-05)
    ).astype(BF16)
    logits = jnp.dot(normed, router_ref[...], preferred_element_type=F32)
    ids = ids_ref[...]
    which = lax.broadcasted_iota(jnp.int32, logits.shape, 1)
    scores = []
    for k in range(ids.shape[1]):
        chosen = jnp.sum(
            jnp.where(ids[:, k : k + 1] == which, logits, 0.0), axis=1, keepdims=True
        )
        scores.append(1.0 / (1.0 + jnp.exp(-chosen)))
    total = functools.reduce(lambda a, b: a + b, scores)
    gate = jnp.zeros((blk, 1), F32)
    mine = jnp.zeros((blk, 1), F32)
    for k, score in enumerate(scores):
        hit = ids[:, k : k + 1] == e
        gate = gate + jnp.where(hit, score / total, 0.0)
        mine = mine + jnp.where(hit, 1.0, 0.0)
    row_i = lax.broadcasted_iota(jnp.int32, (blk, blk), 0)
    col_i = lax.broadcasted_iota(jnp.int32, (blk, blk), 1)
    mine_t = jnp.broadcast_to(mine, (blk, blk)).T
    gate_t = jnp.broadcast_to(gate, (blk, blk)).T
    before = jnp.where(row_i < col_i, 1.0, 0.0).astype(BF16)
    rank = jnp.dot(mine_t.astype(BF16), before, preferred_element_type=F32)
    pick = jnp.where(
        (rank.astype(jnp.int32) == row_i) & (mine_t > 0.5), 1.0, 0.0
    )[:cap]
    comb = pick * gate_t[:cap]
    comb_hi = comb.astype(BF16)
    comb_lo = (comb - comb_hi.astype(F32)).astype(BF16)
    rows_buf[s, :, :width_d] = jnp.dot(
        pick.astype(BF16), normed, preferred_element_type=F32
    ).astype(BF16)
    rows_buf[s, :, width_d : width_d + blk] = comb_hi
    rows_buf[s, :, width_d + blk : width_d + 2 * blk] = comb_lo

    pl.semaphore_wait(barrier, n - 1 + chips)

    def forward(b):
        @pl.when((b <= s) & (s < n - 1))
        def _():
            send_rows(b, 0).start()

        @pl.when((b >= s) & (s > 0))
        def _():
            send_rows(b, 1).start()

    forward(s)

    lower = row_i >= col_i
    for h in range(heads):
        lanes = slice(h * dh, (h + 1) * dh)
        g = jnp.broadcast_to(decay_ref[h : h + 1, :], (blk, blk))
        cum = jnp.sum(jnp.where(lower, g, 0.0), axis=1, keepdims=True)
        last = cum[blk - 1 : blk, :]
        scaled = k_ref[:, lanes].astype(F32) * jnp.exp(last - cum)
        local = jnp.dot(
            scaled.T, v_ref[:, lanes].astype(F32), precision=EXACT, preferred_element_type=F32
        )
        states[s, h, :dh, :] = local.astype(BF16)
        states[s, h, dh:, :] = jnp.broadcast_to(jnp.exp(last), (16, dh)).astype(BF16)

    @pl.loop(0, n)
    def _(j):
        @pl.when(j > s)
        def _():
            send_state(j, s).start()

    carried[...] = jnp.zeros_like(carried)

    @pl.loop(0, n)
    def _(j):
        @pl.when(j < s)
        def _():
            send_state(j, j).wait_recv()
            for h in range(heads):
                carried[h] = (
                    states[j, h, dh : dh + 16, :].astype(F32)[0:1, :] * carried[h]
                    + states[j, h, :dh, :].astype(F32)
                )

    for h in range(heads):
        lanes = slice(h * dh, (h + 1) * dh)
        g = jnp.broadcast_to(decay_ref[h : h + 1, :], (blk, blk))
        cum = jnp.sum(jnp.where(lower, g, 0.0), axis=1, keepdims=True)
        diff = cum - jnp.broadcast_to(cum, (blk, blk)).T
        weight = jnp.where(lower, jnp.exp(jnp.where(lower, diff, 0.0)), 0.0)
        q = q_ref[:, lanes]
        sc = (
            lax.dot_general(
                q, k_ref[:, lanes], (((1,), (1,)), ((), ())), preferred_element_type=F32
            )
            * weight
        )
        mixed = jnp.dot(
            sc, v_ref[:, lanes].astype(F32), precision=EXACT, preferred_element_type=F32
        ) + jnp.exp(cum) * jnp.dot(
            q.astype(F32), carried[h], precision=EXACT, preferred_element_type=F32
        )
        mixed = mixed * lax.rsqrt(jnp.mean(mixed * mixed, axis=-1, keepdims=True) + 1e-06)
        attn_buf[s, :, lanes] = mixed.astype(BF16)

    @pl.loop(0, n)
    def _(j):
        @pl.when(j != s)
        def _():
            send_attn(j, s).start()

    load_up.wait()
    load_down.wait()

    near = jnp.minimum(s, n - 1 - s)
    toward = jnp.where(s > n - 1 - s, -1, 1)

    def block_of(t):
        alternate = s + jnp.where(t % 2 == 1, -((t + 1) // 2), t // 2)
        return jnp.where(t <= 2 * near, alternate, s + toward * (t - near))

    def arrive(t):
        b = block_of(t)
        send_rows(b, 0).wait_recv()
        forward(b)

    up_tile = tile_of(up.shape[1], 384)
    down_tile = tile_of(width_d, 512)

    def compute(t, b):
        x = rows_buf[b, :, :width_d]
        for c in range(0, up.shape[1], up_tile):
            z = jnp.dot(x, up[:, c : c + up_tile], preferred_element_type=F32)
            hidden[:, c : c + up_tile] = (z / (1.0 + jnp.exp(-z))).astype(BF16)
        hi = rows_buf[b, :, width_d : width_d + blk]
        lo = rows_buf[b, :, width_d + blk : width_d + 2 * blk]
        pair = jnp.concatenate([hi, lo], axis=0).astype(F32).T.astype(BF16)
        hid = hidden[...]

        @pl.when(t > 0)
        def _():
            send_attn(b, b).wait_recv()

        proj = lax.dot_general(
            attn_buf[b], ow_ref[...], (((1,), (1,)), ((), ())), preferred_element_type=F32
        )
        for c in range(0, width_d, down_tile):
            o = jnp.dot(hid, down[:, c : c + down_tile], preferred_element_type=F32).astype(BF16)
            both = jnp.concatenate([o, o], axis=0)
            y = jnp.dot(pair, both, preferred_element_type=F32).astype(BF16)
            for g in range(n_exp):
                stage[t, g % 2, g // 2, :, c : c + down_tile] = y[g * own : (g + 1) * own]
        if cols % 128 == 0:
            at = pl.ds(pl.multiple_of(s * cols, 128), cols)
            for g in range(n_exp):
                part = stage[t, g % 2, g // 2, :, at].astype(F32)
                stage[t, g % 2, g // 2, :, at] = (part + proj[g * own : (g + 1) * own]).astype(BF16)
        else:
            for j in range(n):

                @pl.when(s == j)
                def _():
                    at = slice(j * cols, (j + 1) * cols)
                    for g in range(n_exp):
                        part = stage[t, g % 2, g // 2, :, at].astype(F32)
                        stage[t, g % 2, g // 2, :, at] = (
                            part + proj[g * own : (g + 1) * own]
                        ).astype(BF16)

    def across_cores(t):
        send_core(t).wait_recv()

        @pl.loop(0, chips)
        def _(g):
            half_buf[t, g] = (
                stage[t, core, g].astype(F32) + core_buf[t, g].astype(F32)
            ).astype(BF16)

            @pl.when(g != chip)
            def _():
                send_chip(t, g, chip).start()

    def across_chips(t):
        chip_buf[t, chip] = half_buf[t, chip]

        @pl.loop(0, chips)
        def _(g):
            @pl.when(g != chip)
            def _():
                send_chip(t, g, g).wait_recv()

        acc = chip_buf[t, 0].astype(F32)
        for g in range(1, chips):
            acc = acc + chip_buf[t, g].astype(F32)
        fin_send[t] = acc.astype(BF16)

        @pl.when(t > 0)
        def _():
            send_fin(t, block_of(t), s).start()

    @pl.loop(0, n)
    def _(t):
        @pl.when(t % 2 == 1)
        def _():
            arrive(t)

            @pl.when(t + 1 <= 2 * near)
            def _():
                arrive(t + 1)

        @pl.when((t % 2 == 0) & (t > 2 * near) & (t > 0))
        def _():
            arrive(t)

        compute(t, block_of(t))
        send_core(t).start()

        @pl.when(t > 0)
        def _():
            across_chips(t - 1)

        across_cores(t)

    across_chips(n - 1)
    picked = jnp.where(
        lax.broadcasted_iota(jnp.int32, (max(own, 16), blk), 1)
        == lax.broadcasted_iota(jnp.int32, (max(own, 16), blk), 0) + e * own,
        1.0,
        0.0,
    ).astype(BF16)
    base = jnp.dot(picked, res_ref[...], preferred_element_type=F32)[:own]
    fin_buf[s] = fin_send[0]

    @pl.loop(0, n)
    def _(j):
        @pl.when(j != s)
        def _():
            send_fin(0, j, j).wait_recv()

    acc = fin_buf[0].astype(F32)
    for j in range(1, n):
        acc = acc + fin_buf[j].astype(F32)
    out_ref[...] = (base + acc).astype(BF16)

    @pl.loop(0, n)
    def _(j):
        @pl.when((j <= s) & (s < n - 1))
        def _():
            send_rows(j, 0).wait_send()

        @pl.when((j >= s) & (s > 0))
        def _():
            send_rows(j, 1).wait_send()

        @pl.when(j > s)
        def _():
            send_state(j, s).wait_send()

        @pl.when(j != s)
        def _():
            send_attn(j, s).wait_send()

        send_core(j).wait_send()

        @pl.when(j > 0)
        def _():
            send_fin(j, block_of(j), s).wait_send()

        @pl.loop(0, chips)
        def _(g):
            @pl.when(g != chip)
            def _():
                send_chip(j, g, chip).wait_send()


def shards(
    queries,
    key_matrix,
    values,
    log_decay,
    residual,
    out_weight,
    router,
    expert_ids,
    up_weight,
    down_weight,
):
    n = lax.axis_size("seq")
    n_exp = lax.axis_size("exp")
    blk, width_d = residual.shape
    heads = log_decay.shape[0]
    feats = queries.shape[1]
    dh = feats // heads
    cap = 3 * blk * expert_ids.shape[1] // (2 * n_exp)
    cap = -(-cap // 16) * 16
    own = blk // n_exp
    chips = n_exp // 2
    ff = up_weight.shape[2]
    dma = pltpu.SemaphoreType.DMA
    vmem = pl.BlockSpec(memory_space=pltpu.VMEM)
    hbm = pl.BlockSpec(memory_space=pl.ANY)
    return pl.pallas_call(
        functools.partial(layer, n, n_exp, cap),
        out_shape=jax.ShapeDtypeStruct((own, width_d), BF16),
        in_specs=[vmem] * 8 + [hbm] * 2,
        out_specs=vmem,
        scratch_shapes=[
            pltpu.VMEM((width_d, ff), BF16),
            pltpu.VMEM((ff, width_d), BF16),
            pltpu.VMEM((n, cap, width_d + 2 * blk), BF16),
            pltpu.VMEM((cap, ff), BF16),
            pltpu.VMEM((n, heads, dh + 16, dh), BF16),
            pltpu.VMEM((heads, dh, dh), F32),
            pltpu.VMEM((n, blk, feats), BF16),
            pltpu.VMEM((n, 2, chips, own, width_d), BF16),
            pltpu.VMEM((n, chips, own, width_d), BF16),
            pltpu.VMEM((n, chips, own, width_d), BF16),
            pltpu.VMEM((n, chips, own, width_d), BF16),
            pltpu.VMEM((n, own, width_d), BF16),
            pltpu.VMEM((n, own, width_d), BF16),
            dma((2,)),
            dma((2, n)),
            dma((n,)),
            dma((n,)),
            dma((n,)),
            dma((n,)),
            dma((n,)),
            dma((n,)),
            dma((n,)),
            dma((n, chips)),
            dma((n, chips)),
            dma((n,)),
            dma((n,)),
        ],
        compiler_params=pltpu.CompilerParams(
            collective_id=0,
            has_side_effects=True,
            vmem_limit_bytes=56 * 2**20,
        ),
    )(
        queries,
        key_matrix,
        values,
        log_decay,
        residual,
        out_weight,
        router,
        expert_ids,
        up_weight,
        down_weight,
    )


def solution(mesh):
    in_specs = (
        P("seq", "exp"),
        P("seq", "exp"),
        P("seq", "exp"),
        P("exp", "seq"),
        P("seq", None),
        P("seq", "exp"),
        P(),
        P("seq", None),
        P("exp", None, "seq"),
        P("exp", "seq", None),
    )
    out_specs = P(("seq", "exp"), None)
    return jax.shard_map(shards, mesh=mesh, in_specs=in_specs, out_specs=out_specs, check_vma=False)
```

```python
import functools

import jax
import jax.numpy as jnp
from jax import lax
from jax.experimental import pallas as pl
from jax.experimental.pallas import tpu as pltpu
from jax.sharding import PartitionSpec as P

MESH = pl.DeviceIdType.MESH
F32 = jnp.float32
BF16 = jnp.bfloat16
EXACT = lax.Precision.HIGHEST


def tile_of(size, most):
    for width in range(most, 127, -128):
        if size % width == 0:
            return width
    return size


def layer(
    n,
    n_exp,
    cap,
    q_ref,
    k_ref,
    v_ref,
    decay_ref,
    res_ref,
    ow_ref,
    router_ref,
    ids_ref,
    up_hbm,
    down_hbm,
    out_ref,
    up,
    down,
    rows_buf,
    hidden,
    states,
    carried,
    attn_buf,
    stage,
    core_buf,
    half_buf,
    chip_buf,
    fin_send,
    fin_buf,
    load_sem,
    rows_s,
    rows_r,
    st_s,
    st_r,
    at_s,
    at_r,
    core_s,
    core_r,
    chip_s,
    chip_r,
    fin_s,
    fin_r,
):
    s = lax.axis_index("seq")
    e = lax.axis_index("exp")
    core = e % 2
    chip = e // 2
    chips = n_exp // 2
    partner = chip * 2 + 1 - core
    blk, width_d = res_ref.shape
    own = blk // n_exp
    heads = decay_ref.shape[0]
    dh = q_ref.shape[1] // heads
    cols = ow_ref.shape[0]

    load_up = pltpu.make_async_copy(up_hbm.at[0], up, load_sem.at[0])
    load_down = pltpu.make_async_copy(down_hbm.at[0], down, load_sem.at[1])
    load_up.start()
    load_down.start()

    barrier = pltpu.get_barrier_semaphore()

    @pl.loop(0, n)
    def _(j):
        @pl.when(j != s)
        def _():
            pl.semaphore_signal(barrier, inc=1, device_id=(j, e), device_id_type=MESH)

    @pl.loop(0, chips)
    def _(g):
        @pl.when(g != chip)
        def _():
            pl.semaphore_signal(
                barrier, inc=1, device_id=(s, g * 2 + core), device_id_type=MESH
            )

    pl.semaphore_signal(barrier, inc=1, device_id=(s, partner), device_id_type=MESH)

    def send_rows(b, way):
        return pltpu.make_async_remote_copy(
            src_ref=rows_buf.at[b],
            dst_ref=rows_buf.at[b],
            send_sem=rows_s.at[way, b],
            recv_sem=rows_r.at[b],
            device_id=((s + 1) % n if way == 0 else (s + n - 1) % n, e),
            device_id_type=MESH,
        )

    def send_state(to, slot):
        return pltpu.make_async_remote_copy(
            src_ref=states.at[slot],
            dst_ref=states.at[slot],
            send_sem=st_s.at[to],
            recv_sem=st_r.at[slot],
            device_id=(to, e),
            device_id_type=MESH,
        )

    def send_attn(to, slot):
        return pltpu.make_async_remote_copy(
            src_ref=attn_buf.at[slot],
            dst_ref=attn_buf.at[slot],
            send_sem=at_s.at[to],
            recv_sem=at_r.at[slot],
            device_id=(to, e),
            device_id_type=MESH,
        )

    def send_core(t):
        return pltpu.make_async_remote_copy(
            src_ref=stage.at[t, 1 - core],
            dst_ref=core_buf.at[t],
            send_sem=core_s.at[t],
            recv_sem=core_r.at[t],
            device_id=(s, partner),
            device_id_type=MESH,
        )

    def send_chip(t, to, slot):
        return pltpu.make_async_remote_copy(
            src_ref=half_buf.at[t, to],
            dst_ref=chip_buf.at[t, slot],
            send_sem=chip_s.at[t, to],
            recv_sem=chip_r.at[t, slot],
            device_id=(s, to * 2 + core),
            device_id_type=MESH,
        )

    def send_fin(t, to, slot):
        return pltpu.make_async_remote_copy(
            src_ref=fin_send.at[t],
            dst_ref=fin_buf.at[slot],
            send_sem=fin_s.at[t],
            recv_sem=fin_r.at[slot],
            device_id=(to, e),
            device_id_type=MESH,
        )

    stream = res_ref[...].astype(F32)
    normed = (
        stream * lax.rsqrt(jnp.mean(stream * stream, axis=-1, keepdims=True) + 1e-05)
    ).astype(BF16)
    logits = lax.dot_general(
        router_ref[...], normed, (((1,), (1,)), ((), ())), preferred_element_type=F32
    )
    ids = ids_ref[...]
    which = lax.broadcasted_iota(jnp.int32, logits.shape, 0)
    scores = []
    for k in range(ids.shape[0]):
        chosen = jnp.sum(
            jnp.where(ids[k : k + 1, :] == which, logits, 0.0), axis=0, keepdims=True
        )
        scores.append(1.0 / (1.0 + jnp.exp(-chosen)))
    total = functools.reduce(lambda a, b: a + b, scores)
    gate = jnp.zeros((1, blk), F32)
    mine = jnp.zeros((1, blk), F32)
    for k, score in enumerate(scores):
        hit = ids[k : k + 1, :] == e
        gate = gate + jnp.where(hit, score / total, 0.0)
        mine = mine + jnp.where(hit, 1.0, 0.0)
    row_i = lax.broadcasted_iota(jnp.int32, (blk, blk), 0)
    col_i = lax.broadcasted_iota(jnp.int32, (blk, blk), 1)
    mine_t = jnp.broadcast_to(mine, (blk, blk))
    gate_t = jnp.broadcast_to(gate, (blk, blk))
    before = jnp.where(row_i < col_i, 1.0, 0.0).astype(BF16)
    rank = jnp.dot(mine_t.astype(BF16), before, preferred_element_type=F32)
    pick = jnp.where(
        (rank.astype(jnp.int32) == row_i) & (mine_t > 0.5), 1.0, 0.0
    )[:cap]
    comb = pick * gate_t[:cap]
    comb_hi = comb.astype(BF16)
    comb_lo = (comb - comb_hi.astype(F32)).astype(BF16)
    rows_buf[s, :, :width_d] = jnp.dot(
        pick.astype(BF16), normed, preferred_element_type=F32
    ).astype(BF16)
    rows_buf[s, :, width_d : width_d + blk] = comb_hi
    rows_buf[s, :, width_d + blk : width_d + 2 * blk] = comb_lo

    pl.semaphore_wait(barrier, n - 1 + chips)

    def forward(b):
        @pl.when((b <= s) & (s < n - 1))
        def _():
            send_rows(b, 0).start()

        @pl.when((b >= s) & (s > 0))
        def _():
            send_rows(b, 1).start()

    forward(s)

    lower = row_i >= col_i
    for h in range(heads):
        lanes = slice(h * dh, (h + 1) * dh)
        g = jnp.broadcast_to(decay_ref[h : h + 1, :], (blk, blk))
        cum = jnp.sum(jnp.where(lower, g, 0.0), axis=1, keepdims=True)
        last = cum[blk - 1 : blk, :]
        scaled = k_ref[:, lanes].astype(F32) * jnp.exp(last - cum)
        local = jnp.dot(
            scaled.T, v_ref[:, lanes].astype(F32), precision=EXACT, preferred_element_type=F32
        )
        states[s, h, :dh, :] = local.astype(BF16)
        states[s, h, dh:, :] = jnp.broadcast_to(jnp.exp(last), (16, dh)).astype(BF16)

    @pl.loop(0, n)
    def _(j):
        @pl.when(j > s)
        def _():
            send_state(j, s).start()

    up_tile = tile_of(up.shape[1], 384)
    down_tile = tile_of(width_d, 512)

    def expand(b):
        x = rows_buf[b, :, :width_d]
        for c in range(0, up.shape[1], up_tile):
            z = jnp.dot(x, up[:, c : c + up_tile], preferred_element_type=F32)
            hidden[:, c : c + up_tile] = (z / (1.0 + jnp.exp(-z))).astype(BF16)

    load_up.wait()
    expand(s)

    carried[...] = jnp.zeros_like(carried)

    @pl.loop(0, n)
    def _(j):
        @pl.when(j < s)
        def _():
            send_state(j, j).wait_recv()
            for h in range(heads):
                carried[h] = (
                    states[j, h, dh : dh + 16, :].astype(F32)[0:1, :] * carried[h]
                    + states[j, h, :dh, :].astype(F32)
                )

    for h in range(heads):
        lanes = slice(h * dh, (h + 1) * dh)
        g = jnp.broadcast_to(decay_ref[h : h + 1, :], (blk, blk))
        cum = jnp.sum(jnp.where(lower, g, 0.0), axis=1, keepdims=True)
        diff = cum - jnp.broadcast_to(cum, (blk, blk)).T
        weight = jnp.where(lower, jnp.exp(jnp.where(lower, diff, 0.0)), 0.0)
        q = q_ref[:, lanes]
        sc = (
            lax.dot_general(
                q, k_ref[:, lanes], (((1,), (1,)), ((), ())), preferred_element_type=F32
            )
            * weight
        )
        mixed = jnp.dot(
            sc, v_ref[:, lanes].astype(F32), precision=EXACT, preferred_element_type=F32
        ) + jnp.exp(cum) * jnp.dot(
            q.astype(F32), carried[h], precision=EXACT, preferred_element_type=F32
        )
        mixed = mixed * lax.rsqrt(jnp.mean(mixed * mixed, axis=-1, keepdims=True) + 1e-06)
        attn_buf[s, :, lanes] = mixed.astype(BF16)

    @pl.loop(0, n)
    def _(j):
        @pl.when(j != s)
        def _():
            send_attn(j, s).start()

    load_down.wait()

    near = jnp.minimum(s, n - 1 - s)
    toward = jnp.where(s > n - 1 - s, -1, 1)

    def block_of(t):
        alternate = s + jnp.where(t % 2 == 1, -((t + 1) // 2), t // 2)
        return jnp.where(t <= 2 * near, alternate, s + toward * (t - near))

    def arrive(t):
        b = block_of(t)
        send_rows(b, 0).wait_recv()
        forward(b)

    def compute(t, b):
        @pl.when(t > 0)
        def _():
            expand(b)
            across_cores(t - 1)

        hi = rows_buf[b, :, width_d : width_d + blk]
        lo = rows_buf[b, :, width_d + blk : width_d + 2 * blk]
        pair = jnp.concatenate([hi, lo], axis=0).astype(F32).T.astype(BF16)
        hid = hidden[...]

        @pl.when(t > 0)
        def _():
            send_attn(b, b).wait_recv()

        proj = lax.dot_general(
            attn_buf[b], ow_ref[...], (((1,), (1,)), ((), ())), preferred_element_type=F32
        )
        for c in range(0, width_d, down_tile):
            o = jnp.dot(hid, down[:, c : c + down_tile], preferred_element_type=F32).astype(BF16)
            both = jnp.concatenate([o, o], axis=0)
            y = jnp.dot(pair, both, preferred_element_type=F32).astype(BF16)
            for g in range(n_exp):
                stage[t, g % 2, g // 2, :, c : c + down_tile] = y[g * own : (g + 1) * own]
        if cols % 128 == 0:
            at = pl.ds(pl.multiple_of(s * cols, 128), cols)
            for g in range(n_exp):
                part = stage[t, g % 2, g // 2, :, at].astype(F32)
                stage[t, g % 2, g // 2, :, at] = (part + proj[g * own : (g + 1) * own]).astype(BF16)
        else:
            for j in range(n):

                @pl.when(s == j)
                def _():
                    at = slice(j * cols, (j + 1) * cols)
                    for g in range(n_exp):
                        part = stage[t, g % 2, g // 2, :, at].astype(F32)
                        stage[t, g % 2, g // 2, :, at] = (
                            part + proj[g * own : (g + 1) * own]
                        ).astype(BF16)

    def across_cores(t):
        send_core(t).wait_recv()

        @pl.loop(0, chips)
        def _(g):
            half_buf[t, g] = (
                stage[t, core, g].astype(F32) + core_buf[t, g].astype(F32)
            ).astype(BF16)

            @pl.when(g != chip)
            def _():
                send_chip(t, g, chip).start()

    def across_chips(t):
        chip_buf[t, chip] = half_buf[t, chip]

        @pl.loop(0, chips)
        def _(g):
            @pl.when(g != chip)
            def _():
                send_chip(t, g, g).wait_recv()

        acc = chip_buf[t, 0].astype(F32)
        for g in range(1, chips):
            acc = acc + chip_buf[t, g].astype(F32)
        fin_send[t] = acc.astype(BF16)

        @pl.when(t > 0)
        def _():
            send_fin(t, block_of(t), s).start()

    @pl.loop(0, n)
    def _(t):
        @pl.when(t % 2 == 1)
        def _():
            arrive(t)

            @pl.when(t + 1 <= 2 * near)
            def _():
                arrive(t + 1)

        @pl.when((t % 2 == 0) & (t > 2 * near) & (t > 0))
        def _():
            arrive(t)

        compute(t, block_of(t))
        send_core(t).start()

        @pl.when((t > 0) & (t < n - 1))
        def _():
            across_chips(t - 1)

    across_cores(n - 1)
    across_chips(n - 2)
    across_chips(n - 1)
    picked = jnp.where(
        lax.broadcasted_iota(jnp.int32, (max(own, 16), blk), 1)
        == lax.broadcasted_iota(jnp.int32, (max(own, 16), blk), 0) + e * own,
        1.0,
        0.0,
    ).astype(BF16)
    base = jnp.dot(picked, res_ref[...], preferred_element_type=F32)[:own]
    fin_buf[s] = fin_send[0]

    @pl.loop(0, n)
    def _(j):
        @pl.when(j != s)
        def _():
            send_fin(0, j, j).wait_recv()

    acc = fin_buf[0].astype(F32)
    for j in range(1, n):
        acc = acc + fin_buf[j].astype(F32)
    out_ref[...] = (base + acc).astype(BF16)

    @pl.loop(0, n)
    def _(j):
        @pl.when((j <= s) & (s < n - 1))
        def _():
            send_rows(j, 0).wait_send()

        @pl.when((j >= s) & (s > 0))
        def _():
            send_rows(j, 1).wait_send()

        @pl.when(j > s)
        def _():
            send_state(j, s).wait_send()

        @pl.when(j != s)
        def _():
            send_attn(j, s).wait_send()

        send_core(j).wait_send()

        @pl.when(j > 0)
        def _():
            send_fin(j, block_of(j), s).wait_send()

        @pl.loop(0, chips)
        def _(g):
            @pl.when(g != chip)
            def _():
                send_chip(j, g, chip).wait_send()


def shards(
    queries,
    key_matrix,
    values,
    log_decay,
    residual,
    out_weight,
    router,
    expert_ids,
    up_weight,
    down_weight,
):
    n = lax.axis_size("seq")
    n_exp = lax.axis_size("exp")
    blk, width_d = residual.shape
    heads = log_decay.shape[0]
    feats = queries.shape[1]
    dh = feats // heads
    cap = 3 * blk * expert_ids.shape[1] // (2 * n_exp)
    cap = -(-cap // 16) * 16
    own = blk // n_exp
    chips = n_exp // 2
    ff = up_weight.shape[2]
    dma = pltpu.SemaphoreType.DMA
    vmem = pl.BlockSpec(memory_space=pltpu.VMEM)
    hbm = pl.BlockSpec(memory_space=pl.ANY)
    return pl.pallas_call(
        functools.partial(layer, n, n_exp, cap),
        out_shape=jax.ShapeDtypeStruct((own, width_d), BF16),
        in_specs=[vmem] * 8 + [hbm] * 2,
        out_specs=vmem,
        scratch_shapes=[
            pltpu.VMEM((width_d, ff), BF16),
            pltpu.VMEM((ff, width_d), BF16),
            pltpu.VMEM((n, cap, width_d + 2 * blk), BF16),
            pltpu.VMEM((cap, ff), BF16),
            pltpu.VMEM((n, heads, dh + 16, dh), BF16),
            pltpu.VMEM((heads, dh, dh), F32),
            pltpu.VMEM((n, blk, feats), BF16),
            pltpu.VMEM((n, 2, chips, own, width_d), BF16),
            pltpu.VMEM((n, chips, own, width_d), BF16),
            pltpu.VMEM((n, chips, own, width_d), BF16),
            pltpu.VMEM((n, chips, own, width_d), BF16),
            pltpu.VMEM((n, own, width_d), BF16),
            pltpu.VMEM((n, own, width_d), BF16),
            dma((2,)),
            dma((2, n)),
            dma((n,)),
            dma((n,)),
            dma((n,)),
            dma((n,)),
            dma((n,)),
            dma((n,)),
            dma((n,)),
            dma((n, chips)),
            dma((n, chips)),
            dma((n,)),
            dma((n,)),
        ],
        compiler_params=pltpu.CompilerParams(
            collective_id=0,
            has_side_effects=True,
            vmem_limit_bytes=56 * 2**20,
        ),
    )(
        queries,
        key_matrix,
        values,
        log_decay,
        residual,
        out_weight,
        router.T,
        expert_ids.T,
        up_weight,
        down_weight,
    )


def solution(mesh):
    in_specs = (
        P("seq", "exp"),
        P("seq", "exp"),
        P("seq", "exp"),
        P("exp", "seq"),
        P("seq", None),
        P("seq", "exp"),
        P(),
        P("seq", None),
        P("exp", None, "seq"),
        P("exp", "seq", None),
    )
    out_specs = P(("seq", "exp"), None)
    return jax.shard_map(shards, mesh=mesh, in_specs=in_specs, out_specs=out_specs, check_vma=False)
```

```python
import functools

import jax
import jax.numpy as jnp
from jax import lax
from jax.experimental import pallas as pl
from jax.experimental.pallas import tpu as pltpu
from jax.sharding import PartitionSpec as P

MESH = pl.DeviceIdType.MESH
F32 = jnp.float32
BF16 = jnp.bfloat16
EXACT = lax.Precision.HIGHEST


def tile_of(size, most):
    for width in range(most, 127, -128):
        if size % width == 0:
            return width
    return size


def layer(
    n,
    n_exp,
    cap,
    q_ref,
    k_ref,
    v_ref,
    decay_ref,
    res_ref,
    ow_ref,
    router_ref,
    ids_ref,
    up_hbm,
    down_hbm,
    out_ref,
    up,
    down,
    rows_buf,
    hidden,
    states,
    carried,
    attn_buf,
    stage,
    core_buf,
    half_buf,
    chip_buf,
    fin_send,
    fin_buf,
    load_sem,
    rows_s,
    rows_r,
    st_s,
    st_r,
    at_s,
    at_r,
    core_s,
    core_r,
    chip_s,
    chip_r,
    fin_s,
    fin_r,
):
    s = lax.axis_index("seq")
    e = lax.axis_index("exp")
    core = e % 2
    chip = e // 2
    chips = n_exp // 2
    partner = chip * 2 + 1 - core
    blk, width_d = res_ref.shape
    own = blk // n_exp
    heads = decay_ref.shape[0]
    dh = q_ref.shape[1] // heads
    cols = ow_ref.shape[0]

    load_up = pltpu.make_async_copy(up_hbm.at[0], up, load_sem.at[0])
    load_down = pltpu.make_async_copy(down_hbm.at[0], down, load_sem.at[1])
    load_up.start()
    load_down.start()

    barrier = pltpu.get_barrier_semaphore()

    @pl.loop(0, n)
    def _(j):
        @pl.when(j != s)
        def _():
            pl.semaphore_signal(barrier, inc=1, device_id=(j, e), device_id_type=MESH)

    @pl.loop(0, chips)
    def _(g):
        @pl.when(g != chip)
        def _():
            pl.semaphore_signal(
                barrier, inc=1, device_id=(s, g * 2 + core), device_id_type=MESH
            )

    pl.semaphore_signal(barrier, inc=1, device_id=(s, partner), device_id_type=MESH)

    def send_rows(b, way):
        return pltpu.make_async_remote_copy(
            src_ref=rows_buf.at[b],
            dst_ref=rows_buf.at[b],
            send_sem=rows_s.at[way, b],
            recv_sem=rows_r.at[b],
            device_id=((s + 1) % n if way == 0 else (s + n - 1) % n, e),
            device_id_type=MESH,
        )

    def send_state(to, slot):
        return pltpu.make_async_remote_copy(
            src_ref=states.at[slot],
            dst_ref=states.at[slot],
            send_sem=st_s.at[to],
            recv_sem=st_r.at[slot],
            device_id=(to, e),
            device_id_type=MESH,
        )

    def send_attn(to, slot):
        return pltpu.make_async_remote_copy(
            src_ref=attn_buf.at[slot],
            dst_ref=attn_buf.at[slot],
            send_sem=at_s.at[to],
            recv_sem=at_r.at[slot],
            device_id=(to, e),
            device_id_type=MESH,
        )

    def send_core(t):
        return pltpu.make_async_remote_copy(
            src_ref=stage.at[t, 1 - core],
            dst_ref=core_buf.at[t],
            send_sem=core_s.at[t],
            recv_sem=core_r.at[t],
            device_id=(s, partner),
            device_id_type=MESH,
        )

    def send_chip(t, to, slot):
        return pltpu.make_async_remote_copy(
            src_ref=half_buf.at[t, to],
            dst_ref=chip_buf.at[t, slot],
            send_sem=chip_s.at[t, to],
            recv_sem=chip_r.at[t, slot],
            device_id=(s, to * 2 + core),
            device_id_type=MESH,
        )

    def send_fin(t, to, slot):
        return pltpu.make_async_remote_copy(
            src_ref=fin_send.at[t],
            dst_ref=fin_buf.at[slot],
            send_sem=fin_s.at[t],
            recv_sem=fin_r.at[slot],
            device_id=(to, e),
            device_id_type=MESH,
        )

    stream = res_ref[...].astype(F32)
    normed = (
        stream * lax.rsqrt(jnp.mean(stream * stream, axis=-1, keepdims=True) + 1e-05)
    ).astype(BF16)
    logits = lax.dot_general(
        router_ref[...], normed, (((1,), (1,)), ((), ())), preferred_element_type=F32
    )
    ids = ids_ref[...]
    which = lax.broadcasted_iota(jnp.int32, logits.shape, 0)
    scores = []
    for k in range(ids.shape[0]):
        chosen = jnp.sum(
            jnp.where(ids[k : k + 1, :] == which, logits, 0.0), axis=0, keepdims=True
        )
        scores.append(1.0 / (1.0 + jnp.exp(-chosen)))
    total = functools.reduce(lambda a, b: a + b, scores)
    gate = jnp.zeros((1, blk), F32)
    mine = jnp.zeros((1, blk), F32)
    for k, score in enumerate(scores):
        hit = ids[k : k + 1, :] == e
        gate = gate + jnp.where(hit, score / total, 0.0)
        mine = mine + jnp.where(hit, 1.0, 0.0)
    row_i = lax.broadcasted_iota(jnp.int32, (blk, blk), 0)
    col_i = lax.broadcasted_iota(jnp.int32, (blk, blk), 1)
    mine_t = jnp.broadcast_to(mine, (blk, blk))
    gate_t = jnp.broadcast_to(gate, (blk, blk))
    before = jnp.where(row_i < col_i, 1.0, 0.0).astype(BF16)
    rank = jnp.dot(mine_t.astype(BF16), before, preferred_element_type=F32)
    pick = jnp.where(
        (rank.astype(jnp.int32) == row_i) & (mine_t > 0.5), 1.0, 0.0
    )[:cap]
    comb = pick * gate_t[:cap]
    comb_hi = comb.astype(BF16)
    comb_lo = (comb - comb_hi.astype(F32)).astype(BF16)
    rows_buf[s, :, :width_d] = jnp.dot(
        pick.astype(BF16), normed, preferred_element_type=F32
    ).astype(BF16)
    rows_buf[s, :, width_d : width_d + blk] = comb_hi
    rows_buf[s, :, width_d + blk : width_d + 2 * blk] = comb_lo

    pl.semaphore_wait(barrier, n - 1 + chips)

    def forward(b):
        @pl.when((b <= s) & (s < n - 1))
        def _():
            send_rows(b, 0).start()

        @pl.when((b >= s) & (s > 0))
        def _():
            send_rows(b, 1).start()

    forward(s)

    lower = row_i >= col_i
    for h in range(heads):
        lanes = slice(h * dh, (h + 1) * dh)
        g = jnp.broadcast_to(decay_ref[h : h + 1, :], (blk, blk))
        cum = jnp.sum(jnp.where(lower, g, 0.0), axis=1, keepdims=True)
        last = cum[blk - 1 : blk, :]
        scaled = k_ref[:, lanes].astype(F32) * jnp.exp(last - cum)
        local = jnp.dot(
            scaled.T, v_ref[:, lanes].astype(F32), precision=EXACT, preferred_element_type=F32
        )
        states[s, h, :dh, :] = local.astype(BF16)
        states[s, h, dh:, :] = jnp.broadcast_to(jnp.exp(last), (16, dh)).astype(BF16)

    @pl.loop(0, n)
    def _(j):
        @pl.when(j > s)
        def _():
            send_state(j, s).start()

    up_tile = tile_of(up.shape[1], 1152)
    down_tile = tile_of(width_d, 1024)

    def expand(b):
        x = rows_buf[b, :, :width_d]
        for c in range(0, up.shape[1], up_tile):
            z = jnp.dot(x, up[:, c : c + up_tile], preferred_element_type=F32)
            hidden[:, c : c + up_tile] = (z / (1.0 + jnp.exp(-z))).astype(BF16)

    load_up.wait()
    expand(s)

    carried[...] = jnp.zeros_like(carried)

    @pl.loop(0, n)
    def _(j):
        @pl.when(j < s)
        def _():
            send_state(j, j).wait_recv()
            for h in range(heads):
                carried[h] = (
                    states[j, h, dh : dh + 16, :].astype(F32)[0:1, :] * carried[h]
                    + states[j, h, :dh, :].astype(F32)
                )

    for h in range(heads):
        lanes = slice(h * dh, (h + 1) * dh)
        g = jnp.broadcast_to(decay_ref[h : h + 1, :], (blk, blk))
        cum = jnp.sum(jnp.where(lower, g, 0.0), axis=1, keepdims=True)
        diff = cum - jnp.broadcast_to(cum, (blk, blk)).T
        weight = jnp.where(lower, jnp.exp(jnp.where(lower, diff, 0.0)), 0.0)
        q = q_ref[:, lanes]
        sc = (
            lax.dot_general(
                q, k_ref[:, lanes], (((1,), (1,)), ((), ())), preferred_element_type=F32
            )
            * weight
        )
        mixed = jnp.dot(
            sc, v_ref[:, lanes].astype(F32), precision=EXACT, preferred_element_type=F32
        ) + jnp.exp(cum) * jnp.dot(
            q.astype(F32), carried[h], precision=EXACT, preferred_element_type=F32
        )
        mixed = mixed * lax.rsqrt(jnp.mean(mixed * mixed, axis=-1, keepdims=True) + 1e-06)
        attn_buf[s, :, lanes] = mixed.astype(BF16)

    @pl.loop(0, n)
    def _(j):
        @pl.when(j != s)
        def _():
            send_attn(j, s).start()

    load_down.wait()

    near = jnp.minimum(s, n - 1 - s)
    toward = jnp.where(s > n - 1 - s, -1, 1)

    def block_of(t):
        alternate = s + jnp.where(t % 2 == 1, -((t + 1) // 2), t // 2)
        return jnp.where(t <= 2 * near, alternate, s + toward * (t - near))

    def arrive(t):
        b = block_of(t)
        send_rows(b, 0).wait_recv()
        forward(b)

    def compute(t, b):
        @pl.when(t > 0)
        def _():
            expand(b)
            across_cores(t - 1)

        hi = rows_buf[b, :, width_d : width_d + blk]
        lo = rows_buf[b, :, width_d + blk : width_d + 2 * blk]
        pair = jnp.concatenate([hi, lo], axis=0).astype(F32).T.astype(BF16)
        hid = hidden[...]

        @pl.when(t > 0)
        def _():
            send_attn(b, b).wait_recv()

        proj = lax.dot_general(
            attn_buf[b], ow_ref[...], (((1,), (1,)), ((), ())), preferred_element_type=F32
        )
        for c in range(0, width_d, down_tile):
            o = jnp.dot(hid, down[:, c : c + down_tile], preferred_element_type=F32).astype(BF16)
            both = jnp.concatenate([o, o], axis=0)
            y = jnp.dot(pair, both, preferred_element_type=F32).astype(BF16)
            for g in range(n_exp):
                stage[t, g % 2, g // 2, :, c : c + down_tile] = y[g * own : (g + 1) * own]
        if cols % 128 == 0:
            at = pl.ds(pl.multiple_of(s * cols, 128), cols)
            for g in range(n_exp):
                part = stage[t, g % 2, g // 2, :, at].astype(F32)
                stage[t, g % 2, g // 2, :, at] = (part + proj[g * own : (g + 1) * own]).astype(BF16)
        else:
            for j in range(n):

                @pl.when(s == j)
                def _():
                    at = slice(j * cols, (j + 1) * cols)
                    for g in range(n_exp):
                        part = stage[t, g % 2, g // 2, :, at].astype(F32)
                        stage[t, g % 2, g // 2, :, at] = (
                            part + proj[g * own : (g + 1) * own]
                        ).astype(BF16)

    def across_cores(t):
        send_core(t).wait_recv()

        @pl.loop(0, chips)
        def _(g):
            half_buf[t, g] = (
                stage[t, core, g].astype(F32) + core_buf[t, g].astype(F32)
            ).astype(BF16)

            @pl.when(g != chip)
            def _():
                send_chip(t, g, chip).start()

    def across_chips(t):
        chip_buf[t, chip] = half_buf[t, chip]

        @pl.loop(0, chips)
        def _(g):
            @pl.when(g != chip)
            def _():
                send_chip(t, g, g).wait_recv()

        acc = chip_buf[t, 0].astype(F32)
        for g in range(1, chips):
            acc = acc + chip_buf[t, g].astype(F32)
        fin_send[t] = acc.astype(BF16)

        @pl.when(t > 0)
        def _():
            send_fin(t, block_of(t), s).start()

    @pl.loop(0, n)
    def _(t):
        @pl.when(t % 2 == 1)
        def _():
            arrive(t)

            @pl.when(t + 1 <= 2 * near)
            def _():
                arrive(t + 1)

        @pl.when((t % 2 == 0) & (t > 2 * near) & (t > 0))
        def _():
            arrive(t)

        compute(t, block_of(t))
        send_core(t).start()

        @pl.when((t > 0) & (t < n - 1))
        def _():
            across_chips(t - 1)

    across_cores(n - 1)
    across_chips(n - 2)
    across_chips(n - 1)
    picked = jnp.where(
        lax.broadcasted_iota(jnp.int32, (max(own, 16), blk), 1)
        == lax.broadcasted_iota(jnp.int32, (max(own, 16), blk), 0) + e * own,
        1.0,
        0.0,
    ).astype(BF16)
    base = jnp.dot(picked, res_ref[...], preferred_element_type=F32)[:own]
    fin_buf[s] = fin_send[0]

    @pl.loop(0, n)
    def _(j):
        @pl.when(j != s)
        def _():
            send_fin(0, j, j).wait_recv()

    acc = fin_buf[0].astype(F32)
    for j in range(1, n):
        acc = acc + fin_buf[j].astype(F32)
    out_ref[...] = (base + acc).astype(BF16)

    @pl.loop(0, n)
    def _(j):
        @pl.when((j <= s) & (s < n - 1))
        def _():
            send_rows(j, 0).wait_send()

        @pl.when((j >= s) & (s > 0))
        def _():
            send_rows(j, 1).wait_send()

        @pl.when(j > s)
        def _():
            send_state(j, s).wait_send()

        @pl.when(j != s)
        def _():
            send_attn(j, s).wait_send()

        send_core(j).wait_send()

        @pl.when(j > 0)
        def _():
            send_fin(j, block_of(j), s).wait_send()

        @pl.loop(0, chips)
        def _(g):
            @pl.when(g != chip)
            def _():
                send_chip(j, g, chip).wait_send()


def shards(
    queries,
    key_matrix,
    values,
    log_decay,
    residual,
    out_weight,
    router,
    expert_ids,
    up_weight,
    down_weight,
):
    n = lax.axis_size("seq")
    n_exp = lax.axis_size("exp")
    blk, width_d = residual.shape
    heads = log_decay.shape[0]
    feats = queries.shape[1]
    dh = feats // heads
    cap = 3 * blk * expert_ids.shape[1] // (2 * n_exp)
    cap = -(-cap // 16) * 16
    own = blk // n_exp
    chips = n_exp // 2
    ff = up_weight.shape[2]
    dma = pltpu.SemaphoreType.DMA
    vmem = pl.BlockSpec(memory_space=pltpu.VMEM)
    hbm = pl.BlockSpec(memory_space=pl.ANY)
    return pl.pallas_call(
        functools.partial(layer, n, n_exp, cap),
        out_shape=jax.ShapeDtypeStruct((own, width_d), BF16),
        in_specs=[vmem] * 8 + [hbm] * 2,
        out_specs=vmem,
        scratch_shapes=[
            pltpu.VMEM((width_d, ff), BF16),
            pltpu.VMEM((ff, width_d), BF16),
            pltpu.VMEM((n, cap, width_d + 2 * blk), BF16),
            pltpu.VMEM((cap, ff), BF16),
            pltpu.VMEM((n, heads, dh + 16, dh), BF16),
            pltpu.VMEM((heads, dh, dh), F32),
            pltpu.VMEM((n, blk, feats), BF16),
            pltpu.VMEM((n, 2, chips, own, width_d), BF16),
            pltpu.VMEM((n, chips, own, width_d), BF16),
            pltpu.VMEM((n, chips, own, width_d), BF16),
            pltpu.VMEM((n, chips, own, width_d), BF16),
            pltpu.VMEM((n, own, width_d), BF16),
            pltpu.VMEM((n, own, width_d), BF16),
            dma((2,)),
            dma((2, n)),
            dma((n,)),
            dma((n,)),
            dma((n,)),
            dma((n,)),
            dma((n,)),
            dma((n,)),
            dma((n,)),
            dma((n, chips)),
            dma((n, chips)),
            dma((n,)),
            dma((n,)),
        ],
        compiler_params=pltpu.CompilerParams(
            collective_id=0,
            has_side_effects=True,
            vmem_limit_bytes=56 * 2**20,
        ),
    )(
        queries,
        key_matrix,
        values,
        log_decay,
        residual,
        out_weight,
        router.T,
        expert_ids.T,
        up_weight,
        down_weight,
    )


def solution(mesh):
    in_specs = (
        P("seq", "exp"),
        P("seq", "exp"),
        P("seq", "exp"),
        P("exp", "seq"),
        P("seq", None),
        P("seq", "exp"),
        P(),
        P("seq", None),
        P("exp", None, "seq"),
        P("exp", "seq", None),
    )
    out_specs = P(("seq", "exp"), None)
    return jax.shard_map(shards, mesh=mesh, in_specs=in_specs, out_specs=out_specs, check_vma=False)
```
